128 devices in a mesh: prompt: 4 (over y), resp: 32 (over x, z, core).
Axes of the slice: x: 4, y: 4, z: 4, core: 2. Of those that a mesh axis runs over, the one named last changes fastest.
Arguments:
- queries: bfloat16 [16384, 64, 576], P(('prompt', 'resp')), may hold values from -340 to 340
- d_output: bfloat16 [16384, 64, 512], P(('prompt', 'resp')), may hold values from -6 to 6
- resp_latent: bfloat16 [16384, 576], P(('prompt', 'resp')), may hold values from -7 to 7
- prompt_latent: bfloat16 [8, 384, 576], P(None, 'prompt'), may hold values from -6 to 6
- assignment: int32 [128], replicated, may hold values from 0 to 127, each once
- lengths: int32 [128], P(('prompt', 'resp')), may hold values from 32 to 128
Outputs:
- d_prompt_latent: float32 [8, 384, 576], P(None, ('prompt', 'resp'))
- d_resp_latent: float32 [16384, 576], P(('prompt', 'resp'))
The draws below stay inside these ranges and needn't reach their ends.
All inputs are finite; a program needn't handle non-finite values.
Results may differ from the reference program's by a relative error of at most 0.014.
Values may be sent and summed in bfloat16 or wider, within the bound.
A program may use at most 192 MiB of HBM per device.

```python
import jax
import jax.numpy as jnp
from jax import lax

DC = 512
DR = 64
KD = 576
HEADS = 64
QK_DIM = 192
GROUP = 16
RLEN = 128
PLEN = 384
NPROMPT = 8
TOKENS = 16384
DEVICES = 128


def shared_rows(key):
    return jax.random.truncated_normal(key, -6.0, 6.0, (TOKENS, KD), jnp.float32)


def draw_resp_latent(key, part):
    base = shared_rows(key)
    return base.astype(jnp.bfloat16)


def draw_queries(key, part):
    key = jax.random.fold_in(key, 23)
    result = 0.5 * jax.random.truncated_normal(key, -6.0, 6.0, (TOKENS, HEADS, KD), jnp.float32)
    return result.astype(jnp.bfloat16)


def touch_ends(values, stream_key, smallest, top_value):
    index_at = [jax.random.randint(jax.random.fold_in(stream_key, axis), (), 0, length) for axis, length in enumerate(values.shape)]
    longest = values.shape.index(max(values.shape))
    neighbour = index_at[:longest] + [(index_at[longest] + 1) % values.shape[longest]] + index_at[longest + 1:]
    return values.at[tuple(index_at)].set(smallest).at[tuple(neighbour)].set(top_value)


def block_levels(own_key, shape, pieces, smallest, top_value):
    level, own = 1.0, jax.random.fold_in(own_key, 6)
    for dim, shards_of in pieces:
        heights = jnp.exp(jax.random.uniform(jax.random.fold_in(own, dim), (shards_of,), jnp.float32, smallest / len(pieces), top_value / len(pieces)))
        level = level * jnp.repeat(heights, shape[dim] // shards_of).reshape([-1 if axis == dim else 1 for axis in range(len(shape))])
    return level


def scatter_about(own_key, dims, scale, most, shards=(), dtype=jnp.bfloat16):
    drawn = jax.random.normal(own_key, dims, jnp.float32) * scale
    if len(shards) > 0:
        drawn = block_levels(own_key, dims, shards, -0.22, 0.18) * drawn
    return jnp.clip(drawn, min=-most, max=most).astype(dtype)


def setup_inputs(seed: int = 0) -> dict:
    splits = jax.random.split(jax.random.key(seed), 7)
    queries = draw_queries(jax.random.fold_in(splits[6], 71), 0)
    d_output = scatter_about(splits[1], (TOKENS, HEADS, DC), 1.0, 6.0, ((0, 128),))
    resp_latent = draw_resp_latent(jax.random.fold_in(splits[6], 71), 0)
    prompt_latent = scatter_about(splits[3], (NPROMPT, PLEN, KD), 1.0, 6.0, ((1, 4),))
    assignment = jax.random.permutation(splits[4], DEVICES).astype(jnp.int32)
    lengths = touch_ends(jax.random.randint(splits[5], (DEVICES,), RLEN // 4, RLEN + 1), jax.random.fold_in(splits[5], 1), RLEN // 4, RLEN).astype(jnp.int32)
    return {"queries": queries, "d_output": d_output, "resp_latent": resp_latent, "prompt_latent": prompt_latent, "assignment": assignment, "lengths": lengths}


def attend_grads(queries, d_output, keys, length):
    rows = queries.shape[0]
    total = keys.shape[0]
    scale = QK_DIM ** -0.5
    scores = jnp.einsum("thk,sk->ths", queries.astype(jnp.float32), keys.astype(jnp.float32)) * scale
    position = jnp.arange(rows)[:, None]
    key_pos = jnp.arange(total)[None, :] - (total - rows)
    allowed = key_pos <= position
    scores = jnp.where(allowed[:, None, :], scores, -jnp.inf)
    top = jnp.max(scores, axis=-1, keepdims=True)
    expo = jnp.exp(scores - top)
    probs = expo / jnp.sum(expo, axis=-1, keepdims=True)
    probs_b = probs.astype(jnp.bfloat16)
    values = keys[:, :DC]
    output = jnp.einsum("ths,sc->thc", probs_b.astype(jnp.float32), values.astype(jnp.float32))
    live = jnp.arange(rows) < length
    grads = jnp.where(live[:, None, None], d_output, jnp.zeros_like(d_output))
    dprobs = jnp.einsum("thc,sc->ths", grads.astype(jnp.float32), values.astype(jnp.float32))
    delta = jnp.sum(grads.astype(jnp.float32) * output, axis=-1)
    dscores = (probs * (dprobs - delta[..., None])).astype(jnp.bfloat16)
    dkeys = scale * jnp.einsum("ths,thk->sk", dscores.astype(jnp.float32), queries.astype(jnp.float32))
    dvalues = jnp.einsum("ths,thc->sc", probs_b.astype(jnp.float32), grads.astype(jnp.float32))
    return dkeys + jnp.pad(dvalues, ((0, 0), (0, DR)))


def reference(queries, d_output, resp_latent, prompt_latent, assignment, lengths):
    nprompt = prompt_latent.shape[0]
    query_blocks = queries.reshape(DEVICES, RLEN, HEADS, KD)
    grad_blocks = d_output.reshape(DEVICES, RLEN, HEADS, DC)
    own_blocks = resp_latent.reshape(DEVICES, RLEN, KD)
    prompt_ids = (assignment // GROUP).astype(jnp.int32)

    def step(carry, inputs):
        block_q, block_g, block_own, block_prompt, length = inputs
        context = lax.dynamic_index_in_dim(prompt_latent, block_prompt, 0, keepdims=False)
        keys = jnp.concatenate([context, block_own], axis=0)
        dkeys = attend_grads(block_q, block_g, keys, length)
        onehot = (jnp.arange(nprompt) == block_prompt).astype(jnp.float32)
        carry = carry + onehot[:, None, None] * dkeys[None, :PLEN]
        return carry, dkeys[PLEN:]

    init = jnp.zeros((nprompt, PLEN, KD), jnp.float32)
    d_prompt, d_resp = lax.scan(step, init, (query_blocks, grad_blocks, own_blocks, prompt_ids, lengths))
    return d_prompt, d_resp.reshape(TOKENS, KD)
```

```python
import functools
import math

import jax
import jax.numpy as jnp
from jax import lax
from jax.experimental import pallas as pl
from jax.experimental.pallas import tpu as pltpu
from jax.sharding import PartitionSpec as P

BF = jnp.bfloat16
F32 = jnp.float32
DC = 512
KD = 576
HEADS = 64
GROUP = 16
RLEN = 128
PLEN = 384
NPROMPT = 8
SCALE = 192 ** -0.5
EXP2_SCALE = SCALE * math.log2(math.e)
MASKED = -1e38
NY, NR = 4, 32
NDEV = NY * NR
SHARD = PLEN // NY
OWN = PLEN // NDEV
KEYS = PLEN + RLEN
G = 4
COLS = G * RLEN
STEPS = HEADS // G
W = 4
MESH = pl.DeviceIdType.MESH


def dot(a, b, on):
    return lax.dot_general(a, b, (on, ((), ())), preferred_element_type=F32)


NN = ((1,), (0,))
NT = ((1,), (1,))


def coords(device):
    return (device // NR, lax.rem(device, NR))


def kernel(
    q_hbm, do_hbm, prompt_hbm, resp_ref, assign_ref, assign_row, len_ref,
    dprompt_ref, dresp_ref,
    q, do_v, do_t, prompt, keys, sendk, s0, s1, d0, d1, p_ref, ds_ref, acc,
    rows, msg32, msg, recv, pick, summed,
    load_sem, do_sem, prompt_sem, ksend_sem, krecv_sem, msend_sem, mrecv_sem,
):
    y = lax.axis_index("prompt")
    r = lax.axis_index("resp")
    me = y * NR + r

    q_load = pltpu.make_async_copy(q_hbm, q, load_sem)
    prompt_load = pltpu.make_async_copy(prompt_hbm, prompt, prompt_sem)
    prompt_load.start()

    def do_load(g):
        heads = pl.ds(pl.multiple_of(g * 16, 16), 16)
        return pltpu.make_async_copy(do_hbm.at[:, heads], do_v.at[:, heads], do_sem.at[g])

    for g in range(4):
        do_load(g).start()
    q_load.start()

    barrier = pltpu.get_barrier_semaphore()

    def greet(step, carry):
        other = lax.rem(me + step, NDEV)
        pl.semaphore_signal(barrier, inc=1, device_id=coords(other), device_id_type=MESH)
        return carry

    lax.fori_loop(1, NDEV, greet, 0)

    prompt_load.wait()
    keys[pl.ds(pl.multiple_of(y * SHARD, 16), SHARD), :] = prompt[assign_ref[me] // GROUP]
    keys[PLEN:KEYS, :] = resp_ref[...].T
    for k in range(1, NY):
        peer = lax.rem(y + k, NY) * NR + r
        sendk[k - 1] = prompt[assign_ref[peer] // GROUP]

    pl.semaphore_wait(barrier, NDEV - 1)

    def key_copy(k):
        return pltpu.make_async_remote_copy(
            src_ref=sendk.at[k - 1],
            dst_ref=keys.at[pl.ds(pl.multiple_of(y * SHARD, 16), SHARD), :],
            send_sem=ksend_sem.at[k - 1],
            recv_sem=krecv_sem.at[k - 1],
            device_id=(lax.rem(y + k, NY), r),
            device_id_type=MESH,
        )

    def key_arrival(k):
        source = lax.rem(y + NY - k, NY)
        return pltpu.make_async_remote_copy(
            src_ref=sendk.at[k - 1],
            dst_ref=keys.at[pl.ds(pl.multiple_of(source * SHARD, 16), SHARD), :],
            send_sem=ksend_sem.at[k - 1],
            recv_sem=krecv_sem.at[k - 1],
            device_id=(lax.rem(y + k, NY), r),
            device_id_type=MESH,
        )

    for k in (2, 1, 3):
        key_copy(k).start()

    def turn(g, carry):
        do_load(g).wait()
        h0 = pl.multiple_of(g * 16, 16)
        x = jnp.concatenate(
            [jnp.swapaxes(do_v[pl.ds(t * 16, 16), pl.ds(h0, 16), :], 0, 1) for t in range(8)], axis=1
        )
        for h in range(16):
            do_t[h0 + h] = x[h].T
        return carry

    lax.fori_loop(0, 4, turn, 0)

    src = lax.broadcasted_iota(jnp.int32, (NDEV, NDEV * 16), 0)
    lane = lax.broadcasted_iota(jnp.int32, (NDEV, NDEV * 16), 1)
    spread = (src == lane // 16).astype(BF)
    pids = jnp.broadcast_to(assign_row[...] // GROUP, (8, NDEV)).astype(BF)
    pid_lane = dot(pids, spread, NN)[0:1]
    row = lax.broadcasted_iota(jnp.int32, (NDEV, NDEV * 16), 0)
    hit = (pid_lane == (row & 7).astype(F32)) & ((row // 8) == (lane & 15))
    pick[...] = hit.astype(BF)

    q_load.wait()
    for k in (1, 2, 3):
        key_arrival(k).wait_recv()

    def qcat(i):
        return jnp.concatenate([q[i * G + h] for h in range(G)], axis=1)

    def dcat(i):
        return jnp.concatenate([do_t[i * G + h] for h in range(G)], axis=1)

    def products(i, s, d):
        s[...] = dot(keys[...], qcat(i), NN)
        d[...] = dot(keys[:, :DC], dcat(i), NN)

    def soft(i, s_ref, d_ref):
        key_pos = lax.broadcasted_iota(jnp.int32, (RLEN, RLEN), 0)
        token = lax.broadcasted_iota(jnp.int32, (RLEN, RLEN), 1)
        allowed = key_pos <= token
        live = lax.broadcasted_iota(jnp.int32, (1, RLEN), 1) < len_ref[0]
        for h in range(G):
            cs = slice(h * RLEN, (h + 1) * RLEN)
            s = s_ref[:, cs]
            s = jnp.concatenate([s[:PLEN], jnp.where(allowed, s[PLEN:], MASKED)], axis=0)
            top = jnp.max(s, axis=0, keepdims=True)
            e = jnp.exp2((s - top) * EXP2_SCALE)
            dp = d_ref[:, cs]
            inv = 1.0 / jnp.sum(e, axis=0, keepdims=True)
            delta = jnp.sum(e * dp, axis=0, keepdims=True) * inv
            inv = jnp.where(live, inv, 0.0)
            p_ref[i, :, cs] = (e * inv).astype(BF)
            ds_ref[i, :, cs] = (e * (inv * SCALE) * (dp - delta)).astype(BF)

    last = STEPS - 1
    products(0, s0, d0)

    def attend(j, carry):
        i = 2 * j
        products(i + 1, s1, d1)
        soft(i, s0, d0)
        products(jnp.minimum(i + 2, last), s0, d0)
        soft(i + 1, s1, d1)
        return carry

    lax.fori_loop(0, STEPS // 2, attend, 0)

    acc[...] = jnp.zeros_like(acc)

    def gradients(j, carry):
        qc = jnp.concatenate([qcat(W * j + w) for w in range(W)], axis=1)
        dc = jnp.concatenate([dcat(W * j + w) for w in range(W)], axis=1)
        ds = jnp.concatenate([ds_ref[W * j + w] for w in range(W)], axis=1)
        p = jnp.concatenate([p_ref[W * j + w] for w in range(W)], axis=1)
        a = dot(qc, ds, NT)
        b = dot(dc, p, NT)
        acc[0:DC, :] += a[:DC] + b
        acc[DC:KD, :] += a[DC:]
        return carry

    lax.fori_loop(0, STEPS // W, gradients, 0)

    for c in range(5):
        rows[c] = acc[c * 128:(c + 1) * 128, 0:PLEN].T
    msg32[pl.ds(15, NDEV, stride=16), :] = jnp.zeros((NDEV, 128), F32)
    for i in range(OWN):
        for c in range(5):
            msg32[pl.ds(i * 5 + c, NDEV, stride=16), :] = rows[c, pl.ds(i, NDEV, stride=OWN), :]
    msg[...] = msg32[...].reshape(NDEV, 16, 128).astype(BF)

    def send(step, carry):
        other = lax.rem(me + step, NDEV)
        pltpu.make_async_remote_copy(
            src_ref=msg.at[other], dst_ref=recv.at[me],
            send_sem=msend_sem, recv_sem=mrecv_sem,
            device_id=coords(other), device_id_type=MESH,
        ).start()
        return carry

    lax.fori_loop(1, NDEV, send, 0)
    recv[me] = msg[me]
    dresp_ref[...] = acc[0:KD, PLEN:KEYS]

    whole = pltpu.make_async_remote_copy(
        src_ref=msg.at[pl.ds(0, NDEV - 1)], dst_ref=recv.at[pl.ds(0, NDEV - 1)],
        send_sem=msend_sem, recv_sem=mrecv_sem,
        device_id=coords(lax.rem(me + 1, NDEV)), device_id_type=MESH,
    )
    whole.wait_recv()
    summed[...] = dot(pick[...], recv[...].reshape(NDEV * 16, 128), NN)
    for i in range(OWN):
        for c in range(5):
            k = i * 5 + c
            width = min(128, KD - c * 128)
            dprompt_ref[i, :, c * 128:c * 128 + width] = summed[k * 8:(k + 1) * 8, 0:width]
    whole.wait_send()
    for k in (1, 2, 3):
        key_copy(k).wait_send()


def body(queries, d_output, resp_latent, prompt_latent, assignment, lengths):
    smem = pl.BlockSpec(memory_space=pltpu.SMEM)
    vmem = pl.BlockSpec(memory_space=pltpu.VMEM)
    hbm = pl.BlockSpec(memory_space=pl.ANY)
    dprompt, dresp = pl.pallas_call(
        kernel,
        out_shape=(
            jax.ShapeDtypeStruct((OWN, NPROMPT, KD), F32),
            jax.ShapeDtypeStruct((KD, RLEN), F32),
        ),
        in_specs=[hbm, hbm, hbm, vmem, smem, vmem, smem],
        out_specs=(vmem, vmem),
        scratch_shapes=[
            pltpu.VMEM((HEADS, KD, RLEN), BF),
            pltpu.VMEM((RLEN, HEADS, DC), BF),
            pltpu.VMEM((HEADS, DC, RLEN), BF),
            pltpu.VMEM((NPROMPT, SHARD, KD), BF),
            pltpu.VMEM((KEYS, KD), BF),
            pltpu.VMEM((NY - 1, SHARD, KD), BF),
            pltpu.VMEM((KEYS, COLS), F32),
            pltpu.VMEM((KEYS, COLS), F32),
            pltpu.VMEM((KEYS, COLS), F32),
            pltpu.VMEM((KEYS, COLS), F32),
            pltpu.VMEM((STEPS, KEYS, COLS), BF),
            pltpu.VMEM((STEPS, KEYS, COLS), BF),
            pltpu.VMEM((640, KEYS), F32),
            pltpu.VMEM((5, PLEN, 128), F32),
            pltpu.VMEM((NDEV * 16, 128), F32),
            pltpu.VMEM((NDEV, 16, 128), BF),
            pltpu.VMEM((NDEV, 16, 128), BF),
            pltpu.VMEM((NDEV, NDEV * 16), BF),
            pltpu.VMEM((NDEV, 128), F32),
            pltpu.SemaphoreType.DMA,
            pltpu.SemaphoreType.DMA((4,)),
            pltpu.SemaphoreType.DMA,
            pltpu.SemaphoreType.DMA((NY - 1,)),
            pltpu.SemaphoreType.DMA((NY - 1,)),
            pltpu.SemaphoreType.DMA,
            pltpu.SemaphoreType.DMA,
        ],
        compiler_params=pltpu.CompilerParams(
            collective_id=0, has_side_effects=True, vmem_limit_bytes=62 * 2 ** 20
        ),
        name="latent_grads",
    )(
        jnp.transpose(queries, (1, 2, 0)), d_output, prompt_latent, resp_latent.T,
        assignment, assignment.reshape(1, NDEV), lengths,
    )
    return jnp.transpose(dprompt, (1, 0, 2)), dresp.T


def solution(mesh):
    in_specs = (
        P(("prompt", "resp"), None, None),
        P(("prompt", "resp"), None, None),
        P(("prompt", "resp"), None),
        P(None, "prompt", None),
        P(),
        P(("prompt", "resp")),
    )
    out_specs = (P(None, ("prompt", "resp"), None), P(("prompt", "resp"), None))
    return jax.shard_map(body, mesh=mesh, in_specs=in_specs, out_specs=out_specs, check_vma=False)
```

```python
import functools
import math

import jax
import jax.numpy as jnp
from jax import lax
from jax.experimental import pallas as pl
from jax.experimental.pallas import tpu as pltpu
from jax.sharding import PartitionSpec as P

BF = jnp.bfloat16
F32 = jnp.float32
DC = 512
KD = 576
HEADS = 64
GROUP = 16
RLEN = 128
PLEN = 384
NPROMPT = 8
SCALE = 192 ** -0.5
EXP2_SCALE = SCALE * math.log2(math.e)
MASKED = -1e38
NY, NR = 4, 32
NDEV = NY * NR
SHARD = PLEN // NY
OWN = PLEN // NDEV
KEYS = PLEN + RLEN
G = 4
COLS = G * RLEN
STEPS = HEADS // G
W = 4
UNROLL = 4
MESH = pl.DeviceIdType.MESH


def dot(a, b, on):
    return lax.dot_general(a, b, (on, ((), ())), preferred_element_type=F32)


NN = ((1,), (0,))
NT = ((1,), (1,))


def kernel(
    q_hbm, do_hbm, prompt_hbm, resp_ref, assign_ref, assign_row, len_ref,
    dprompt_ref, dresp_ref,
    q, do_v, do_t, prompt, keys, sendk, s0, s1, d0, d1, p_ref, ds_ref, acc,
    rows, msg32, msg, recv, pick, summed,
    load_sem, do_sem, prompt_sem, ksend_sem, krecv_sem, msend_sem, mrecv_sem,
    plane_sem, cube_sem, all_sem,
):
    y = lax.axis_index("prompt")
    r = lax.axis_index("resp")
    me = y * NR + r

    q_load = pltpu.make_async_copy(q_hbm, q, load_sem)
    prompt_load = pltpu.make_async_copy(prompt_hbm, prompt, prompt_sem)
    prompt_load.start()

    def do_load(g):
        heads = pl.ds(pl.multiple_of(g * 16, 16), 16)
        return pltpu.make_async_copy(do_hbm.at[:, heads], do_v.at[:, heads], do_sem.at[g])

    for g in range(4):
        do_load(g).start()
    q_load.start()

    x, z, core = r // 8, lax.rem(r // 2, 4), lax.rem(r, 2)
    y_peers = [(lax.rem(y + k, 4), r) for k in (1, 2, 3)]
    x_peers = [(y, lax.rem(x + k, 4) * 8 + z * 2 + core) for k in (1, 2, 3)]
    z_peers = [(y, x * 8 + lax.rem(z + k, 4) * 2 + core) for k in (1, 2, 3)]
    core_peers = [(y, x * 8 + z * 2 + 1 - core)]

    def tell(sem, peers):
        for peer in peers:
            pl.semaphore_signal(sem, inc=1, device_id=peer, device_id_type=MESH)

    barrier = pltpu.get_barrier_semaphore()
    tell(barrier, y_peers + x_peers + z_peers + core_peers)

    prompt_load.wait()
    keys[pl.ds(pl.multiple_of(y * SHARD, 16), SHARD), :] = prompt[assign_ref[me] // GROUP]
    keys[PLEN:KEYS, :] = resp_ref[...].T
    for k in range(1, NY):
        peer = lax.rem(y + k, NY) * NR + r
        sendk[k - 1] = prompt[assign_ref[peer] // GROUP]

    pl.semaphore_wait(barrier, 10)

    def key_copy(k):
        return pltpu.make_async_remote_copy(
            src_ref=sendk.at[k - 1],
            dst_ref=keys.at[pl.ds(pl.multiple_of(y * SHARD, 16), SHARD), :],
            send_sem=ksend_sem.at[k - 1],
            recv_sem=krecv_sem.at[k - 1],
            device_id=(lax.rem(y + k, NY), r),
            device_id_type=MESH,
        )

    def key_arrival(k):
        source = lax.rem(y + NY - k, NY)
        return pltpu.make_async_remote_copy(
            src_ref=sendk.at[k - 1],
            dst_ref=keys.at[pl.ds(pl.multiple_of(source * SHARD, 16), SHARD), :],
            send_sem=ksend_sem.at[k - 1],
            recv_sem=krecv_sem.at[k - 1],
            device_id=(lax.rem(y + k, NY), r),
            device_id_type=MESH,
        )

    for k in (2, 1, 3):
        key_copy(k).start()
    tell(plane_sem, x_peers)

    def turn(g, carry):
        do_load(g).wait()
        h0 = pl.multiple_of(g * 16, 16)
        x = jnp.concatenate(
            [jnp.swapaxes(do_v[pl.ds(t * 16, 16), pl.ds(h0, 16), :], 0, 1) for t in range(8)], axis=1
        )
        for h in range(16):
            do_t[h0 + h] = x[h].T
        return carry

    lax.fori_loop(0, 4, turn, 0)

    src = lax.broadcasted_iota(jnp.int32, (NDEV, NDEV * 16), 0)
    lane = lax.broadcasted_iota(jnp.int32, (NDEV, NDEV * 16), 1)
    spread = (src == lane // 16).astype(BF)
    pids = jnp.broadcast_to(assign_row[...] // GROUP, (8, NDEV)).astype(BF)
    pid_lane = dot(pids, spread, NN)[0:1]
    row = lax.broadcasted_iota(jnp.int32, (NDEV, NDEV * 16), 0)
    hit = (pid_lane == (row & 7).astype(F32)) & ((row // 8) == (lane & 15))
    pick[...] = hit.astype(BF)

    pl.semaphore_wait(plane_sem, 3)
    tell(cube_sem, z_peers)
    q_load.wait()
    for k in (1, 2, 3):
        key_arrival(k).wait_recv()

    def qcat(i):
        return jnp.concatenate([q[i * G + h] for h in range(G)], axis=1)

    def dcat(i):
        return jnp.concatenate([do_t[i * G + h] for h in range(G)], axis=1)

    def scores(i, s):
        s[...] = dot(keys[...], qcat(i), NN)

    def dprobs(i, d):
        d[...] = dot(keys[:, :DC], dcat(i), NN)

    def soft(i, slot, h, s_ref, d_ref):
        key_pos = lax.broadcasted_iota(jnp.int32, (RLEN, RLEN), 0)
        token = lax.broadcasted_iota(jnp.int32, (RLEN, RLEN), 1)
        allowed = key_pos <= token
        live = lax.broadcasted_iota(jnp.int32, (1, RLEN), 1) < len_ref[0]
        cs = slice(h * RLEN, (h + 1) * RLEN)
        s = s_ref[:, cs]
        s = jnp.concatenate([s[:PLEN], jnp.where(allowed, s[PLEN:], MASKED)], axis=0)
        top = jnp.max(s, axis=0, keepdims=True)
        e = jnp.exp2((s - top) * EXP2_SCALE)
        dp = d_ref[:, cs]
        inv = 1.0 / jnp.sum(e, axis=0, keepdims=True)
        delta = jnp.sum(e * dp, axis=0, keepdims=True) * inv
        inv = jnp.where(live, inv, 0.0)
        p_ref[slot, :, cs] = (e * inv).astype(BF)
        ds_ref[slot, :, cs] = (e * (inv * SCALE) * (dp - delta)).astype(BF)

    last = STEPS - 1
    pl.semaphore_wait(cube_sem, 3)
    tell(all_sem, core_peers)
    acc[...] = jnp.zeros_like(acc)

    def grad_k(j, n):
        qc = jnp.concatenate([qcat(j + w) for w in range(n)], axis=1)
        ds = jnp.concatenate([ds_ref[j + w] for w in range(n)], axis=1)
        acc[0:KD, :] += dot(qc, ds, NT)

    def grad_v(j, n):
        dc = jnp.concatenate([dcat(j + w) for w in range(n)], axis=1)
        p = jnp.concatenate([p_ref[j + w] for w in range(n)], axis=1)
        acc[0:DC, :] += dot(dc, p, NT)


    def gradients(i, n):
        qc = jnp.concatenate([qcat(i + w) for w in range(n)], axis=1)
        dc = jnp.concatenate([dcat(i + w) for w in range(n)], axis=1)
        ds = jnp.concatenate([ds_ref[w] for w in range(n)], axis=1)
        p = jnp.concatenate([p_ref[w] for w in range(n)], axis=1)
        a = dot(qc, ds, NT)
        b = dot(dc, p, NT)
        acc[0:DC, :] += a[:DC] + b
        acc[DC:KD, :] += a[DC:]

    def products(i, s, d):
        scores(i, s)
        dprobs(i, d)

    def softs(i, slot, s, d):
        for h in range(G):
            soft(i, slot, h, s, d)

    products(0, s0, d0)

    def attend(j, carry):
        i = 2 * j
        products(i + 1, s1, d1)
        softs(i, 0, s0, d0)
        products(jnp.minimum(i + 2, last), s0, d0)
        softs(i + 1, 1, s1, d1)
        gradients(i, 2)
        return carry

    lax.fori_loop(0, STEPS // 2, attend, 0)

    for c in range(5):
        rows[c] = acc[c * 128:(c + 1) * 128, 0:PLEN].T
    msg32[pl.ds(15, NDEV, stride=16), :] = jnp.zeros((NDEV, 128), F32)
    for i in range(OWN):
        for c in range(5):
            msg32[pl.ds(i * 5 + c, NDEV, stride=16), :] = rows[c, pl.ds(i, NDEV, stride=OWN), :]
    msg[...] = msg32[...].reshape(NDEV, 16, 128).astype(BF)

    pl.semaphore_wait(all_sem, 1)


    def one(oy, other):
        pltpu.make_async_remote_copy(
            src_ref=msg.at[oy * NR + other], dst_ref=recv.at[me],
            send_sem=msend_sem, recv_sem=mrecv_sem,
            device_id=(oy, other), device_id_type=MESH,
        ).start()

    def send(step, carry):
        other = lax.rem(r + step, NR)
        for k in range(NY):
            one(lax.rem(y + k, NY), other)
        return carry

    for k in range(1, NY):
        one(lax.rem(y + k, NY), r)
    lax.fori_loop(1, NR, send, 0)

    recv[me] = msg[me]
    dresp_ref[...] = acc[0:KD, PLEN:KEYS]

    whole = pltpu.make_async_remote_copy(
        src_ref=msg.at[pl.ds(0, NDEV - 1)], dst_ref=recv.at[pl.ds(0, NDEV - 1)],
        send_sem=msend_sem, recv_sem=mrecv_sem,
        device_id=(y, lax.rem(r + 1, NR)), device_id_type=MESH,
    )
    whole.wait_recv()
    summed[...] = dot(pick[...], recv[...].reshape(NDEV * 16, 128), NN)
    for i in range(OWN):
        for c in range(5):
            k = i * 5 + c
            width = min(128, KD - c * 128)
            dprompt_ref[i, :, c * 128:c * 128 + width] = summed[k * 8:(k + 1) * 8, 0:width]
    whole.wait_send()
    for k in (1, 2, 3):
        key_copy(k).wait_send()


def hand_over(dprompt_in, dresp_in, dprompt_out, dresp_out):
    dprompt_out[...] = dprompt_in[...]
    dresp_out[...] = dresp_in[...]


def body(queries, d_output, resp_latent, prompt_latent, assignment, lengths):
    smem = pl.BlockSpec(memory_space=pltpu.SMEM)
    vmem = pl.BlockSpec(memory_space=pltpu.VMEM)
    hbm = pl.BlockSpec(memory_space=pl.ANY)
    dprompt, dresp = pl.pallas_call(
        kernel,
        out_shape=(
            jax.ShapeDtypeStruct((OWN, NPROMPT, KD), F32),
            jax.ShapeDtypeStruct((KD, RLEN), F32),
        ),
        in_specs=[hbm, hbm, hbm, vmem, smem, vmem, smem],
        out_specs=(vmem, vmem),
        scratch_shapes=[
            pltpu.VMEM((HEADS, KD, RLEN), BF),
            pltpu.VMEM((RLEN, HEADS, DC), BF),
            pltpu.VMEM((HEADS, DC, RLEN), BF),
            pltpu.VMEM((NPROMPT, SHARD, KD), BF),
            pltpu.VMEM((KEYS, KD), BF),
            pltpu.VMEM((NY - 1, SHARD, KD), BF),
            pltpu.VMEM((KEYS, COLS), F32),
            pltpu.VMEM((KEYS, COLS), F32),
            pltpu.VMEM((KEYS, COLS), F32),
            pltpu.VMEM((KEYS, COLS), F32),
            pltpu.VMEM((2, KEYS, COLS), BF),
            pltpu.VMEM((2, KEYS, COLS), BF),
            pltpu.VMEM((640, KEYS), F32),
            pltpu.VMEM((5, PLEN, 128), F32),
            pltpu.VMEM((NDEV * 16, 128), F32),
            pltpu.VMEM((NDEV, 16, 128), BF),
            pltpu.VMEM((NDEV, 16, 128), BF),
            pltpu.VMEM((NDEV, NDEV * 16), BF),
            pltpu.VMEM((NDEV, 128), F32),
            pltpu.SemaphoreType.DMA,
            pltpu.SemaphoreType.DMA((4,)),
            pltpu.SemaphoreType.DMA,
            pltpu.SemaphoreType.DMA((NY - 1,)),
            pltpu.SemaphoreType.DMA((NY - 1,)),
            pltpu.SemaphoreType.DMA,
            pltpu.SemaphoreType.DMA,
            pltpu.SemaphoreType.REGULAR,
            pltpu.SemaphoreType.REGULAR,
            pltpu.SemaphoreType.REGULAR,
        ],
        compiler_params=pltpu.CompilerParams(
            collective_id=0, has_side_effects=True, vmem_limit_bytes=62 * 2 ** 20
        ),
        name="latent_grads",
    )(
        jnp.transpose(queries, (1, 2, 0)), d_output, prompt_latent, resp_latent.T,
        assignment, assignment.reshape(1, NDEV), lengths,
    )
    dprompt, dresp = pl.pallas_call(
        hand_over,
        out_shape=(
            jax.ShapeDtypeStruct((OWN, NPROMPT, KD), F32),
            jax.ShapeDtypeStruct((KD, RLEN), F32),
        ),
        in_specs=[vmem, vmem],
        out_specs=(vmem, vmem),
        name="hand_over",
    )(dprompt, dresp)
    return jnp.transpose(dprompt, (1, 0, 2)), dresp.T


def solution(mesh):
    in_specs = (
        P(("prompt", "resp"), None, None),
        P(("prompt", "resp"), None, None),
        P(("prompt", "resp"), None),
        P(None, "prompt", None),
        P(),
        P(("prompt", "resp")),
    )
    out_specs = (P(None, ("prompt", "resp"), None), P(("prompt", "resp"), None))
    return jax.shard_map(body, mesh=mesh, in_specs=in_specs, out_specs=out_specs, check_vma=False)
```
